512 devices in a mesh: row: 16 (over y, z_lo), col: 32 (over x, z_hi, core).
Axes of the slice: x: 4, y: 4, z: 16 (z_hi: 4, z_lo: 4; z = z_hi * 4 + z_lo), core: 2. Of those that a mesh axis runs over, the one named last changes fastest.
Arguments:
- gradient: float32 [5120, 25600], P('row', 'col'), may hold values from -48 to 48
- previous: float32 [5120, 2880], P('row', 'col'), may hold values from -1 to 1
- root: bfloat16 [5120, 2880], P('row', 'col'), may hold values from -2.1 to 2.1
Outputs:
- statistic: float32 [5120, 2880], P('row', 'col')
- preconditioned: float32 [5120, 25600], P('row', 'col')
The draws below stay inside these ranges and needn't reach their ends.
All inputs are finite; a program needn't handle non-finite values.
Results may differ from the reference program's by a relative error of at most 0.005.
Values may be sent and summed in bfloat16 or wider, within the bound.
No kernel may reach another device: no remote copies, remote signals or barrier semaphores. Data moves between devices by JAX's collectives and lax.ppermute only.
A program may use at most 64 MiB of HBM per device.

```python
import math
import jax
import jax.numpy as jnp
from jax import lax

WIDTH = 5120
INTER = 25600
BLOCKS = 16
HALF = 8
BLOCK_ROWS = 320
BAND = 2880
N_COL = 32


def draw_gradient(key, part):
    subkeys = jax.random.split(jax.random.fold_in(key, 11), 3)
    row_scale = jnp.exp(jax.random.uniform(subkeys[0], (WIDTH, 1), jnp.float32, math.log(0.5), math.log(2.0)))
    col_scale = jnp.exp(jax.random.uniform(subkeys[1], (1, INTER), jnp.float32, math.log(0.5), math.log(2.0)))
    shard_place = (jnp.arange(INTER, dtype=jnp.int32)[None, :] // (INTER // N_COL)).astype(jnp.float32)
    shard_scale = jnp.exp(shard_place * (math.log(3.0) / (N_COL - 1)))
    col_scale = col_scale * shard_scale
    rough = jnp.clip(jax.random.normal(subkeys[2], (WIDTH, INTER), jnp.float32), -4.0, 4.0)
    values = rough * row_scale * col_scale
    return values.astype(jnp.float32)


def draw_root(key, part):
    subkeys = jax.random.split(jax.random.fold_in(key, 23), 2)
    spread = 0.5 / math.sqrt(WIDTH)
    noise = jnp.clip(jax.random.normal(subkeys[0], (WIDTH, BAND), jnp.float32), -4.0, 4.0) * spread
    diag_values = jnp.exp(jax.random.uniform(subkeys[1], (WIDTH, 1), jnp.float32, math.log(0.5), math.log(2.0)))
    row_place = jnp.arange(WIDTH, dtype=jnp.int32)[:, None] % BLOCK_ROWS
    col_place = jnp.arange(BAND, dtype=jnp.int32)[None, :]
    on_diagonal = (col_place == row_place).astype(jnp.float32)
    return (noise + on_diagonal * diag_values).astype(jnp.bfloat16)


def block_levels(own_key, extent, pieces, smallest, high):
    loudness = 1.0
    for dim, parts in pieces:
        steps = jax.random.uniform(jax.random.fold_in(jax.random.fold_in(own_key, 6), dim), (parts,), jnp.float32, smallest / len(pieces), high / len(pieces))
        loudness = loudness * jnp.repeat(jnp.exp(steps), extent[dim] // parts).reshape((-1,) + (1,) * (len(extent) - 1 - dim))
    return loudness


def gaussian(rng, shape, deviation, most, cuts=(), held_as=jnp.bfloat16):
    factor_of = block_levels(rng, shape, cuts, -0.22, 0.18) if cuts else 1.0
    entries = jax.random.normal(rng, shape, jnp.float32) * deviation * factor_of
    return jnp.minimum(jnp.maximum(entries, -most), most).astype(held_as)


def setup_inputs(seed: int = 0) -> dict:
    key_of = jax.random.split(jax.random.key(seed), 4)
    return {
        "gradient": draw_gradient(jax.random.fold_in(key_of[3], 71), 0),
        "previous": gaussian(key_of[1], (WIDTH, BAND), 0.2, 1.0, ((0, 16), (1, 32)), jnp.float32),
        "root": draw_root(jax.random.fold_in(key_of[3], 71), 0),
    }


def reference(gradient, previous, root):
    rounded = gradient.astype(jnp.bfloat16).astype(jnp.float32)
    blocks = rounded.reshape(BLOCKS, BLOCK_ROWS, INTER)
    gram_tiles = []
    for offset in range(HALF + 1):
        shifted = jnp.roll(blocks, offset, axis=0)
        gram_tiles.append(jnp.einsum("irn,isn->irs", blocks, shifted, precision=lax.Precision.HIGHEST))
    gram_band = jnp.stack(gram_tiles, axis=2).reshape(WIDTH, BAND)
    statistic = 0.9 * previous + (0.1 / INTER) * gram_band
    root_tiles = root.astype(jnp.float32).reshape(BLOCKS, BLOCK_ROWS, HALF + 1, BLOCK_ROWS)
    applied = jnp.zeros((BLOCKS, BLOCK_ROWS, INTER), jnp.float32)
    for offset in range(HALF + 1):
        shifted = jnp.roll(blocks, offset, axis=0)
        applied = applied + jnp.einsum("irs,isn->irn", root_tiles[:, :, offset, :], shifted, precision=lax.Precision.HIGHEST)
    for offset in range(1, HALF):
        shifted = jnp.roll(blocks, -offset, axis=0)
        mirrored = jnp.roll(root_tiles[:, :, offset, :], -offset, axis=0)
        applied = applied + jnp.einsum("isr,isn->irn", mirrored, shifted, precision=lax.Precision.HIGHEST)
    return statistic, applied.reshape(WIDTH, INTER)
```

```python
import jax
import jax.numpy as jnp
from jax import lax
from jax.sharding import Mesh
from jax.sharding import PartitionSpec as P

INTER = 25600
COL = ("x", "zh", "core")
ALL = ("row",) + COL
TILES = ((0, 0), (0, -1), (6, 4), (-1, -4), (4, 0), (4, -1), (6, 0), (6, -1), (4, -4))


def passed_along(x, axis, by):
    count = lax.axis_size(axis)
    return lax.ppermute(x, axis, [(i, (i + by) % count) for i in range(count)])


def shard_routes(sizes, shard, tile):
    nx, nzh, ncore = sizes
    routes = []
    for c in range(nx * nzh * ncore):
        first, last = c * shard // tile, (c * shard + shard - 1) // tile
        core, rest = divmod(c, nx * nzh)
        x, zh = divmod(rest, nzh)
        place = (x * nzh + zh) * ncore + core
        one, two = TILES[first][0], TILES[last][0]
        routes.append((c, place, one, two, last * tile - c * shard if one != two else shard))
    return routes


def dot(left, right, dims):
    return lax.dot_general(left, right, (dims, ((), ())), preferred_element_type=jnp.float32)


def local(gradient, previous, root):
    rows, shard = previous.shape
    n_row = lax.axis_size("row")
    nx, nzh, ncore = (lax.axis_size(a) for a in COL)
    n_col = nx * nzh * ncore
    routes = shard_routes((nx, nzh, ncore), shard, rows)
    core = lax.axis_index("core")
    col = lax.axis_index(COL)
    cut = jnp.asarray([r[4] for r in routes], jnp.int32)[col]
    held_c = (core * nx + lax.axis_index("x")) * nzh + lax.axis_index("zh")
    held_cut = jnp.asarray([r[4] for r in routes], jnp.int32)[held_c]
    place_in_shard = lax.broadcasted_iota(jnp.int32, (shard, rows), 0)

    g = {0: gradient.astype(jnp.bfloat16)}
    g[-1] = passed_along(g[0], "row", 1)
    g[-4] = passed_along(g[0], "row", 4)
    g[4] = passed_along(g[0], "row", -4)
    g[6] = passed_along(g[-1], "row", -7)

    mine = root.T
    to_use = [
        [((i + r[pick]) % n_row * n_col + r[0], i * n_col + r[1]) for i in range(n_row) for r in routes if pick == 2 or r[2] != r[3]]
        for pick in (2, 3)
    ]
    one = lax.ppermute(mine, ALL, to_use[0])
    two = lax.ppermute(mine, ALL, to_use[1])
    piece = jnp.where(place_in_shard < held_cut, one, two)
    piece = lax.all_to_all(jnp.broadcast_to(piece[None], (nzh,) + piece.shape), "zh", 0, 0, tiled=True)
    piece = lax.all_to_all(jnp.broadcast_to(piece[None], (nx,) + piece.shape), "x", 0, 0, tiled=True)
    other = passed_along(piece, "core", 1)
    root_t = jnp.concatenate(
        [jnp.where(core == 0, piece, other), jnp.where(core == 0, other, piece)], 0
    ).reshape(-1, rows)

    gram = jnp.concatenate(
        [dot(g[b], g[a], ((1,), (1,))).astype(jnp.bfloat16) for a, b in TILES], 0
    )
    half = gram.shape[0] // ncore
    keep = lax.dynamic_slice_in_dim(gram, core * half, half, 0)
    give = lax.dynamic_slice_in_dim(gram, (1 - core) * half, half, 0)
    total = keep.astype(jnp.float32) + passed_along(give, "core", 1).astype(jnp.float32)
    for axis, count in (("x", nx), ("zh", nzh)):
        parts = total.astype(jnp.bfloat16).reshape(count, -1, rows)
        total = lax.all_to_all(parts, axis, 0, 0, tiled=True).astype(jnp.float32).sum(0)
    total = total.astype(jnp.bfloat16)
    home = [[(b, a) for a, b in pairs] for pairs in to_use]
    one = lax.ppermute(total, ALL, home[0])
    two = lax.ppermute(total, ALL, home[1])
    share = jnp.where(place_in_shard < cut, one, two).astype(jnp.float32).T
    statistic = 0.9 * previous + 0.1 / INTER * share

    out = {}
    last = n_row // 2
    for k, (a, b) in enumerate(TILES):
        tile = root_t[k * rows : (k + 1) * rows]
        terms = [(a, dot(tile, g[b], ((0,), (0,))))]
        if 0 < k < last:
            terms.append((b, dot(tile, g[a], ((1,), (0,)))))
        for o, term in terms:
            out[o] = out[o] + term if o in out else term
    applied = out[0]
    for o in (4, -4):
        applied = applied + passed_along(out[o].astype(jnp.bfloat16), "row", o).astype(jnp.float32)
    chained = out[-1] + passed_along(out[6].astype(jnp.bfloat16), "row", 7).astype(jnp.float32)
    applied = applied + passed_along(chained.astype(jnp.bfloat16), "row", -1).astype(jnp.float32)
    return (statistic, applied)


def solution(mesh):
    split = Mesh(mesh.devices.reshape(mesh.shape["row"], 4, 4, 2), ALL)
    spec = P("row", COL)
    return jax.shard_map(
        local, mesh=split, in_specs=(spec,) * 3, out_specs=(spec,) * 2, check_vma=False
    )
```

```python
import functools

import jax
import jax.numpy as jnp
from jax import lax
from jax.experimental import pallas as pl
from jax.experimental.pallas import tpu as pltpu
from jax.sharding import Mesh
from jax.sharding import PartitionSpec as P

INTER = 25600
COL = ("x", "zh", "core")
ALL = ("row",) + COL
TILES = ((0, 0), (0, -1), (6, 4), (-1, -4), (4, 0), (4, -1), (6, 0), (6, -1), (4, -4))
LATE = tuple(k for k, t in enumerate(TILES) if 6 in t)
EARLY = tuple(k for k, t in enumerate(TILES) if 6 not in t)


def passed_along(x, axis, by):
    count = lax.axis_size(axis)
    return lax.ppermute(x, axis, [(i, (i + by) % count) for i in range(count)])


def shard_routes(sizes, shard, tile):
    nx, nzh, ncore = sizes
    routes = []
    for c in range(nx * nzh * ncore):
        first, last = c * shard // tile, (c * shard + shard - 1) // tile
        core, rest = divmod(c, nx * nzh)
        x, zh = divmod(rest, nzh)
        place = (x * nzh + zh) * ncore + core
        one, two = TILES[first][0], TILES[last][0]
        routes.append((c, place, one, two, last * tile - c * shard if one != two else shard))
    return routes


def dot(left, right, dims):
    return lax.dot_general(left, right, (dims, ((), ())), preferred_element_type=jnp.float32)


def call(kernel, outs, args, scratch=(), flops=0):
    moved = sum(a.size * a.dtype.itemsize for a in args)
    return pl.pallas_call(
        kernel,
        out_shape=[jax.ShapeDtypeStruct(s, d) for s, d in outs],
        in_specs=[pl.BlockSpec(memory_space=pltpu.VMEM)] * len(args),
        out_specs=[pl.BlockSpec(memory_space=pltpu.VMEM)] * len(outs),
        scratch_shapes=list(scratch),
        cost_estimate=pl.CostEstimate(flops=flops, bytes_accessed=moved, transcendentals=0),
        compiler_params=pltpu.CompilerParams(vmem_limit_bytes=48 * 2**20),
    )(*args)


def early_gram(g0, gm1, gm4, g4, out):
    held = {0: g0, -1: gm1, -4: gm4, 4: g4}
    for n, k in enumerate(EARLY):
        a, b = TILES[k]
        out[n] = dot(held[b][...], held[a][...], ((1,), (1,))).astype(out.dtype)


def late_gram(g0, gm1, g4, g6, early, keep, give):
    held = {0: g0, -1: gm1, 4: g4, 6: g6}
    core = lax.axis_index("core")
    rows = early.shape[1]
    half = keep.shape[0]

    def put(low, high):
        for k, (a, b) in enumerate(TILES):
            if k in LATE:
                tile = dot(held[b][...], held[a][...], ((1,), (1,)))
            else:
                tile = early[EARLY.index(k)]
            start = k * rows
            if start + rows <= half:
                low[start : start + rows] = tile.astype(low.dtype)
            elif start >= half:
                high[start - half : start - half + rows] = tile.astype(high.dtype)
            else:
                cut = half - start
                low[start:half] = tile[:cut].astype(low.dtype)
                high[: rows - cut] = tile[cut:].astype(high.dtype)

    @pl.when(core == 0)
    def _():
        put(keep, give)

    @pl.when(core == 1)
    def _():
        put(give, keep)


def core_sum(keep, came, *rest):
    outs, total = rest[:-1], rest[-1]
    count = len(outs)
    part = total.shape[0] // count
    me = lax.axis_index("x")
    total[...] = keep[...] + came[...].astype(jnp.float32)
    for s, out in enumerate(outs):
        start = pl.multiple_of(lax.rem(me + s, count) * part, 8)
        out[...] = total[pl.ds(start, part)].astype(out.dtype)


def x_sum(*rest):
    count = (len(rest) - 1) // 2
    ins, outs, total = rest[:count], rest[count:-1], rest[-1]
    part = outs[0].shape[0]
    me = lax.axis_index("zh")
    value = sum(i[...].astype(jnp.float32) for i in ins)
    for q in range(count):
        total[q, :part] = value[q * part : (q + 1) * part]
    for s, out in enumerate(outs):
        out[...] = total[lax.rem(me + s, count), :part].astype(out.dtype)


def assemble(mine, other, g0, gm1, g4, tiles, out6, flat):
    nx, nzh, shard, rows = mine.shape
    x, zh, core = lax.axis_index("x"), lax.axis_index("zh"), lax.axis_index("core")

    def put(parts):
        for b, part in enumerate(parts):
            for p in range(nx):
                for q in range(nzh):
                    c = (b * nx + p) * nzh + q
                    piece = part[lax.rem(p - x + nx, nx), lax.rem(q - zh + nzh, nzh)]
                    flat[c * shard : (c + 1) * shard] = piece.astype(jnp.float32)

    @pl.when(core == 0)
    def _():
        put((mine, other))

    @pl.when(core == 1)
    def _():
        put((other, mine))

    for k in range(len(TILES)):
        tiles[k] = flat[k * rows : (k + 1) * rows].astype(tiles.dtype)
    out6[...] = summed_terms(tiles, {0: g0, -1: gm1, 4: g4}, 6).astype(out6.dtype)


def summed_terms(tiles, held, o):
    total = None
    for k, (a, b) in enumerate(TILES):
        if a == o:
            term = dot(tiles[k], held[b][...], ((0,), (0,)))
            total = term if total is None else total + term
        if b == o and 0 < k < len(TILES) - 1:
            term = dot(tiles[k], held[a][...], ((1,), (0,)))
            total = term if total is None else total + term
    return total


def products(which, tiles, g0, gm1, gm4, g4, g6, *outs):
    held = {0: g0, -1: gm1, -4: gm4, 4: g4, 6: g6}
    for o, out in zip(which, outs):
        out[...] = summed_terms(tiles, held, o).astype(out.dtype)


def local(gradient, previous, root):
    rows, shard = previous.shape
    n_row = lax.axis_size("row")
    nx, nzh, ncore = (lax.axis_size(a) for a in COL)
    n_col = nx * nzh * ncore
    routes = shard_routes((nx, nzh, ncore), shard, rows)
    cuts = jnp.asarray([r[4] for r in routes], jnp.int32)
    cut = cuts[lax.axis_index(COL)]
    held_cut = cuts[lax.axis_index(("core", "x", "zh"))]
    place_in_shard = lax.broadcasted_iota(jnp.int32, (shard, rows), 0)
    bf16, f32 = jnp.bfloat16, jnp.float32
    product = 2 * rows * rows * gradient.shape[1]

    g0 = gradient.astype(bf16)
    gm1 = passed_along(g0, "row", 1)
    gm4 = passed_along(g0, "row", 4)
    g4 = passed_along(g0, "row", -4)
    g6 = passed_along(gm1, "row", -7)

    to_use = [
        [
            ((i + r[pick]) % n_row * n_col + r[0], i * n_col + r[1])
            for i in range(n_row)
            for r in routes
            if pick == 2 or r[2] != r[3]
        ]
        for pick in (2, 3)
    ]
    mine = root.T
    one = lax.ppermute(mine, ALL, to_use[0])
    two = lax.ppermute(mine, ALL, to_use[1])
    piece = jnp.where(place_in_shard < held_cut, one, two)
    piece = jnp.stack([piece] + [passed_along(piece, "zh", -s) for s in range(1, nzh)])
    piece = jnp.stack([piece] + [passed_along(piece, "x", -s) for s in range(1, nx)])
    other = passed_along(piece, "core", 1)

    (early,) = call(
        early_gram, [((len(EARLY), rows, rows), bf16)], (g0, gm1, gm4, g4), flops=len(EARLY) * product
    )
    half = len(TILES) * rows // ncore
    keep, give = call(
        late_gram,
        [((half, rows), f32), ((half, rows), bf16)],
        (g0, gm1, g4, g6, early),
        flops=len(LATE) * product,
    )
    came = passed_along(give, "core", 1)
    part = half // nx
    sent = call(core_sum, [((part, rows), bf16)] * nx, (keep, came), [pltpu.VMEM((half, rows), f32)])
    got = [sent[0]] + [passed_along(sent[s], "x", s) for s in range(1, nx)]
    padded = -(-shard // 8) * 8
    sent = call(x_sum, [((shard, rows), bf16)] * nzh, got, [pltpu.VMEM((nzh, padded, rows), f32)])
    got = [sent[0]] + [passed_along(sent[s], "zh", s) for s in range(1, nzh)]
    total = sum(a.astype(f32) for a in got).astype(bf16)
    home = [[(b, a) for a, b in pairs] for pairs in to_use]
    one = lax.ppermute(total, ALL, home[0])
    two = lax.ppermute(total, ALL, home[1])
    share = jnp.where(place_in_shard < cut, one, two).astype(f32).T
    statistic = 0.9 * previous + 0.1 / INTER * share

    shape = g0.shape
    tiles, out6 = call(
        assemble,
        [((len(TILES), rows, rows), bf16), (shape, bf16)],
        (piece, other, g0, gm1, g4),
        [pltpu.VMEM((len(TILES) * rows, rows), f32)],
        flops=3 * product,
    )
    operands = (tiles, g0, gm1, gm4, g4, g6)
    came6 = passed_along(out6, "row", 7)
    out4, outm4 = call(
        functools.partial(products, (4, -4)), [(shape, bf16)] * 2, operands, flops=5 * product
    )
    came4, camem4 = passed_along(out4, "row", 4), passed_along(outm4, "row", -4)
    outm1, out0 = call(
        functools.partial(products, (-1, 0)), [(shape, f32)] * 2, operands, flops=8 * product
    )
    chained = passed_along((outm1 + came6.astype(f32)).astype(bf16), "row", -1)
    applied = out0 + came4.astype(f32) + camem4.astype(f32) + chained.astype(f32)
    return (statistic, applied)


def solution(mesh):
    split = Mesh(mesh.devices.reshape(mesh.shape["row"], 4, 4, 2), ALL)
    spec = P("row", COL)
    return jax.shard_map(
        local, mesh=split, in_specs=(spec,) * 3, out_specs=(spec,) * 2, check_vma=False
    )
```

```python
import functools

import jax
import jax.numpy as jnp
from jax import lax
from jax.experimental import pallas as pl
from jax.experimental.pallas import tpu as pltpu
from jax.sharding import Mesh
from jax.sharding import PartitionSpec as P

INTER = 25600
COL = ("x", "zh", "core")
ALL = ("row",) + COL
TILES = ((0, 0), (0, -1), (6, 4), (-1, -4), (4, 0), (4, -1), (6, 0), (6, -1), (4, -4))
LATE = tuple(k for k, t in enumerate(TILES) if 6 in t)
HIDES = 10**10
EARLY = tuple(k for k, t in enumerate(TILES) if 6 not in t)


def passed_along(x, axis, by):
    count = lax.axis_size(axis)
    return lax.ppermute(x, axis, [(i, (i + by) % count) for i in range(count)])


def shard_routes(sizes, shard, tile):
    nx, nzh, ncore = sizes
    routes = []
    for c in range(nx * nzh * ncore):
        first, last = c * shard // tile, (c * shard + shard - 1) // tile
        core, rest = divmod(c, nx * nzh)
        x, zh = divmod(rest, nzh)
        place = (x * nzh + zh) * ncore + core
        one, two = TILES[first][0], TILES[last][0]
        routes.append((c, place, one, two, last * tile - c * shard if one != two else shard))
    return routes


def dot(left, right, dims):
    return lax.dot_general(left, right, (dims, ((), ())), preferred_element_type=jnp.float32)


def call(kernel, outs, args, scratch=(), flops=0):
    moved = sum(a.size * a.dtype.itemsize for a in args)
    return pl.pallas_call(
        kernel,
        out_shape=[jax.ShapeDtypeStruct(s, d) for s, d in outs],
        in_specs=[pl.BlockSpec(memory_space=pltpu.VMEM)] * len(args),
        out_specs=[pl.BlockSpec(memory_space=pltpu.VMEM)] * len(outs),
        scratch_shapes=list(scratch),
        cost_estimate=pl.CostEstimate(flops=flops, bytes_accessed=moved, transcendentals=0),
        compiler_params=pltpu.CompilerParams(vmem_limit_bytes=24 * 2**20),
    )(*args)


def early_gram(g0, gm1, gm4, g4, out):
    held = {0: g0, -1: gm1, -4: gm4, 4: g4}
    for n, k in enumerate(EARLY):
        a, b = TILES[k]
        out[n] = dot(held[b][...], held[a][...], ((1,), (1,))).astype(out.dtype)


def late_gram(g0, gm1, g4, g6, early, keep, give, flat):
    held = {0: g0, -1: gm1, 4: g4, 6: g6}
    core = lax.axis_index("core")
    rows = early.shape[1]
    count, full, _ = keep.shape
    shard = len(TILES) * rows // (2 * count)
    for k, (a, b) in enumerate(TILES):
        if k in LATE:
            tile = dot(held[b][...], held[a][...], ((1,), (1,)))
        else:
            tile = early[EARLY.index(k)].astype(jnp.float32)
        flat[k * rows : (k + 1) * rows, :rows] = tile

    def put(outs):
        for q in range(count):
            for b, out in enumerate(outs):
                start = (2 * q + b) * shard
                out[q] = flat[start : start + full].astype(out.dtype)

    @pl.when(core == 0)
    def _():
        put((keep, give))

    @pl.when(core == 1)
    def _():
        put((give, keep))


def partner(zh, core, turn):
    first = (core + turn) % 2 == 0
    near, far = zh + 1 - 2 * (zh % 2), 3 - zh
    if isinstance(core, int):
        return near if first else far
    return jnp.where(first, near, far)


def x_sum(came, keep, send):
    zh, core = lax.axis_index("zh"), lax.axis_index("core")
    for out, who in ((keep, zh), (send, partner(zh, core, 0))):
        for n, q in enumerate((who, partner(who, core, 1))):
            total = sum(came[p, q].astype(jnp.float32) for p in range(came.shape[0]))
            out[n] = total.astype(out.dtype)


def assemble(mine, other, g0, gm1, gm4, g4, g6, tiles, out6, outm1, flat):
    nx, nzh = mine.shape[:2]
    rows = tiles.shape[1]
    shard = flat.shape[0] // (2 * nx * nzh)
    core = lax.axis_index("core")

    def put(parts):
        for x in range(nx):
            for zh in range(nzh):
                for b, part in enumerate(parts):
                    start = ((x * nzh + zh) * 2 + b) * shard
                    flat[start : start + shard] = part[x, zh].astype(jnp.float32)[:shard, :rows]

    @pl.when(core == 0)
    def _():
        put((mine, other))

    @pl.when(core == 1)
    def _():
        put((other, mine))

    for k in range(len(TILES)):
        tiles[k] = flat[k * rows : (k + 1) * rows].astype(tiles.dtype)
    held = {0: g0, -1: gm1, -4: gm4, 4: g4, 6: g6}
    out6[...] = summed_terms(tiles, held, 6).astype(out6.dtype)
    outm1[...] = summed_terms(tiles, held, -1).astype(outm1.dtype)


def summed_terms(tiles, held, o):
    total = None
    for k, (a, b) in enumerate(TILES):
        if a == o:
            term = dot(tiles[k], held[b][...], ((0,), (0,)))
            total = term if total is None else total + term
        if b == o and 0 < k < len(TILES) - 1:
            term = dot(tiles[k], held[a][...], ((1,), (0,)))
            total = term if total is None else total + term
    return total


def products(which, tiles, g0, gm1, gm4, g4, g6, *outs):
    held = {0: g0, -1: gm1, -4: gm4, 4: g4, 6: g6}
    for o, out in zip(which, outs):
        out[...] = summed_terms(tiles, held, o).astype(out.dtype)


def local(gradient, previous, root):
    rows, shard = previous.shape
    n_row = lax.axis_size("row")
    nx, nzh, ncore = (lax.axis_size(a) for a in COL)
    n_col = nx * nzh * ncore
    routes = shard_routes((nx, nzh, ncore), shard, rows)
    cuts = jnp.asarray([r[4] for r in routes], jnp.int32)
    cut = cuts[lax.axis_index(COL)]
    place_in_shard = lax.broadcasted_iota(jnp.int32, (shard, rows), 0)
    bf16, f32 = jnp.bfloat16, jnp.float32
    product = 2 * rows * rows * gradient.shape[1]

    def pairs(pick, place):
        return [
            ((i + r[pick]) % n_row * n_col + r[0], i * n_col + r[place])
            for i in range(n_row)
            for r in routes
            if pick == 2 or r[2] != r[3]
        ]

    mine = root.T
    one = lax.ppermute(mine, ALL, pairs(2, 0))
    two = lax.ppermute(mine, ALL, pairs(3, 0))
    one, two, gradient = lax.optimization_barrier((one, two, gradient))
    piece = jnp.where(place_in_shard < cut, one, two)
    full, lanes = -(-shard // 16) * 16, -(-rows // 128) * 128
    piece = jnp.pad(piece, ((0, full - shard), (0, lanes - rows)))
    turns = [
        [(zh * ncore + c, partner(zh, c, turn) * ncore + c) for zh in range(nzh) for c in range(ncore)]
        for turn in (0, 1)
    ]

    def traded(x, turn):
        return lax.ppermute(x, ("zh", "core"), turns[turn])

    piece = lax.all_to_all(jnp.broadcast_to(piece[None], (nzh,) + piece.shape), "zh", 0, 0, tiled=True)
    piece = lax.all_to_all(jnp.broadcast_to(piece[None], (nx,) + piece.shape), "x", 0, 0, tiled=True)
    pieces = (piece, passed_along(piece, "core", 1))

    g0 = gradient.astype(bf16)
    gm1 = passed_along(g0, "row", 1)
    gm4 = passed_along(g0, "row", 4)
    g4 = passed_along(g0, "row", -4)
    g6 = passed_along(g0, "row", -6)

    g0 = gradient.astype(bf16)
    gm1 = passed_along(g0, "row", 1)
    gm4 = passed_along(g0, "row", 4)
    g4 = passed_along(g0, "row", -4)
    g6 = passed_along(g0, "row", -6)
    blocks = (g0, gm1, gm4, g4, g6)
    chunks = (nx * nzh, full, lanes)
    (early,) = call(early_gram, [((len(EARLY), rows, rows), bf16)], (g0, gm1, gm4, g4), flops=HIDES)
    keep, give = call(
        late_gram,
        [(chunks, bf16)] * 2,
        (g0, gm1, g4, g6, early),
        [pltpu.VMEM((len(TILES) * rows + 8, lanes), f32)],
        flops=HIDES,
    )
    came = passed_along(give, "core", 1)

    shape = g0.shape
    tiles, out6, outm1 = call(
        assemble,
        [((len(TILES), rows, rows), bf16), (shape, bf16), (shape, f32)],
        (*pieces, *blocks),
        [pltpu.VMEM((len(TILES) * rows, rows), f32)],
        flops=7 * product,
    )
    came, tiles, out6 = lax.optimization_barrier((came, tiles, out6))
    chained = (outm1 + passed_along(out6, "row", 7).astype(f32)).astype(bf16)
    camem1 = passed_along(chained, "row", -1)
    out4, outm4 = call(
        functools.partial(products, (4, -4)), [(shape, bf16)] * 2, (tiles, *blocks), flops=5 * product
    )
    came4, camem4 = passed_along(out4, "row", 4), passed_along(outm4, "row", -4)
    (out0,) = call(functools.partial(products, (0,)), [(shape, f32)], (tiles, *blocks), flops=4 * product)

    sent = (keep.astype(f32) + came.astype(f32)).astype(bf16).reshape(nx, nzh, full, lanes)
    got = lax.all_to_all(sent, "x", 0, 0, tiled=True)
    mine, sent = call(x_sum, [((2, full, lanes), bf16)] * 2, (got,))
    mine = (mine.astype(f32) + traded(sent, 0).astype(f32)).astype(bf16)
    total = (mine[0].astype(f32) + traded(mine[1], 1).astype(f32)).astype(bf16)
    total, camem1, came4, camem4 = lax.optimization_barrier((total, camem1, came4, camem4))
    one, two = (lax.ppermute(total, ALL, [(b, a) for a, b in pairs(pick, 0)]) for pick in (2, 3))
    one, two = one[:shard, :rows], two[:shard, :rows]
    share = jnp.where(place_in_shard < cut, one, two).astype(f32).T
    statistic = 0.9 * previous + 0.1 / INTER * share
    applied = out0 + came4.astype(f32) + camem4.astype(f32) + camem1.astype(f32)
    return (statistic, applied)


def solution(mesh):
    split = Mesh(mesh.devices.reshape(mesh.shape["row"], 4, 4, 2), ALL)
    spec = P("row", COL)
    return jax.shard_map(
        local, mesh=split, in_specs=(spec,) * 3, out_specs=(spec,) * 2, check_vma=False
    )
```

```python
import functools

import jax
import jax.numpy as jnp
from jax import lax
from jax.experimental import pallas as pl
from jax.experimental.pallas import tpu as pltpu
from jax.sharding import Mesh
from jax.sharding import PartitionSpec as P

INTER = 25600
COL = ("x", "zh", "core")
ALL = ("row",) + COL
TILES = ((0, 0), (0, -1), (6, 4), (-1, -4), (4, 0), (4, -1), (6, 0), (6, -1), (4, -4))
LATE = tuple(range(1, len(TILES)))
HIDES = 10**10
EARLY = (0,)


def passed_along(x, axis, by):
    count = lax.axis_size(axis)
    return lax.ppermute(x, axis, [(i, (i + by) % count) for i in range(count)])


def shard_routes(sizes, shard, tile):
    nx, nzh, ncore = sizes
    routes = []
    for c in range(nx * nzh * ncore):
        first, last = c * shard // tile, (c * shard + shard - 1) // tile
        core, rest = divmod(c, nx * nzh)
        x, zh = divmod(rest, nzh)
        place = (x * nzh + zh) * ncore + core
        one, two = TILES[first][0], TILES[last][0]
        routes.append((c, place, one, two, last * tile - c * shard if one != two else shard))
    return routes


def dot(left, right, dims):
    return lax.dot_general(left, right, (dims, ((), ())), preferred_element_type=jnp.float32)


def call(kernel, outs, args, scratch=(), flops=0):
    moved = sum(a.size * a.dtype.itemsize for a in args)
    return pl.pallas_call(
        kernel,
        out_shape=[jax.ShapeDtypeStruct(s, d) for s, d in outs],
        in_specs=[pl.BlockSpec(memory_space=pltpu.VMEM)] * len(args),
        out_specs=[pl.BlockSpec(memory_space=pltpu.VMEM)] * len(outs),
        scratch_shapes=list(scratch),
        cost_estimate=pl.CostEstimate(flops=flops, bytes_accessed=moved, transcendentals=0),
        compiler_params=pltpu.CompilerParams(vmem_limit_bytes=24 * 2**20),
    )(*args)


def early_gram(g0, out):
    out[0] = dot(g0[...], g0[...], ((1,), (1,))).astype(out.dtype)


def late_gram(g0, gm1, gm4, g4, g6, early, keep, give, flat):
    held = {0: g0, -1: gm1, -4: gm4, 4: g4, 6: g6}
    core = lax.axis_index("core")
    rows = early.shape[1]
    count, full, _ = keep.shape
    shard = len(TILES) * rows // (2 * count)
    for k, (a, b) in enumerate(TILES):
        if k in LATE:
            tile = dot(held[b][...], held[a][...], ((1,), (1,)))
        else:
            tile = early[EARLY.index(k)].astype(jnp.float32)
        flat[k * rows : (k + 1) * rows, :rows] = tile

    def put(outs):
        for q in range(count):
            for b, out in enumerate(outs):
                start = (2 * q + b) * shard
                out[q] = flat[start : start + full].astype(out.dtype)

    @pl.when(core == 0)
    def _():
        put((keep, give))

    @pl.when(core == 1)
    def _():
        put((give, keep))


def partner(zh, core, turn):
    first = (core + turn) % 2 == 0
    near, far = zh + 1 - 2 * (zh % 2), 3 - zh
    if isinstance(core, int):
        return near if first else far
    return jnp.where(first, near, far)


def x_sum(came, keep, send):
    zh, core = lax.axis_index("zh"), lax.axis_index("core")
    for out, who in ((keep, zh), (send, partner(zh, core, 0))):
        for n, q in enumerate((who, partner(who, core, 1))):
            total = sum(came[p, q].astype(jnp.float32) for p in range(came.shape[0]))
            out[n] = total.astype(out.dtype)


def assemble(mine, other, g0, gm1, g4, tiles, out6, flat):
    nx, nzh = mine.shape[:2]
    rows = tiles.shape[1]
    shard = flat.shape[0] // (2 * nx * nzh)
    core = lax.axis_index("core")

    def put(parts):
        for x in range(nx):
            for zh in range(nzh):
                for b, part in enumerate(parts):
                    start = ((x * nzh + zh) * 2 + b) * shard
                    flat[start : start + shard] = part[x, zh].astype(jnp.float32)[:shard, :rows]

    @pl.when(core == 0)
    def _():
        put((mine, other))

    @pl.when(core == 1)
    def _():
        put((other, mine))

    for k in range(len(TILES)):
        tiles[k] = flat[k * rows : (k + 1) * rows].astype(tiles.dtype)
    out6[...] = summed_terms(tiles, {0: g0, -1: gm1, 4: g4}, 6).astype(out6.dtype)


def summed_terms(tiles, held, o):
    total = None
    for k, (a, b) in enumerate(TILES):
        if a == o:
            term = dot(tiles[k], held[b][...], ((0,), (0,)))
            total = term if total is None else total + term
        if b == o and 0 < k < len(TILES) - 1:
            term = dot(tiles[k], held[a][...], ((1,), (0,)))
            total = term if total is None else total + term
    return total


def products(which, tiles, g0, gm1, gm4, g4, g6, *outs):
    held = {0: g0, -1: gm1, -4: gm4, 4: g4, 6: g6}
    for o, out in zip(which, outs):
        out[...] = summed_terms(tiles, held, o).astype(out.dtype)


def local(gradient, previous, root):
    rows, shard = previous.shape
    n_row = lax.axis_size("row")
    nx, nzh, ncore = (lax.axis_size(a) for a in COL)
    n_col = nx * nzh * ncore
    routes = shard_routes((nx, nzh, ncore), shard, rows)
    cuts = jnp.asarray([r[4] for r in routes], jnp.int32)
    cut = cuts[lax.axis_index(COL)]
    place_in_shard = lax.broadcasted_iota(jnp.int32, (shard, rows), 0)
    bf16, f32 = jnp.bfloat16, jnp.float32
    product = 2 * rows * rows * gradient.shape[1]

    def pairs(pick, place):
        return [
            ((i + r[pick]) % n_row * n_col + r[0], i * n_col + r[place])
            for i in range(n_row)
            for r in routes
            if pick == 2 or r[2] != r[3]
        ]

    mine = root.T
    one = lax.ppermute(mine, ALL, pairs(2, 0))
    two = lax.ppermute(mine, ALL, pairs(3, 0))
    one, two, gradient = lax.optimization_barrier((one, two, gradient))
    piece = jnp.where(place_in_shard < cut, one, two)
    full, lanes = -(-shard // 16) * 16, -(-rows // 128) * 128
    piece = jnp.pad(piece, ((0, full - shard), (0, lanes - rows)))
    turns = [
        [(zh * ncore + c, partner(zh, c, turn) * ncore + c) for zh in range(nzh) for c in range(ncore)]
        for turn in (0, 1)
    ]

    def traded(x, turn):
        return lax.ppermute(x, ("zh", "core"), turns[turn])

    piece = lax.all_to_all(jnp.broadcast_to(piece[None], (nzh,) + piece.shape), "zh", 0, 0, tiled=True)
    piece = lax.all_to_all(jnp.broadcast_to(piece[None], (nx,) + piece.shape), "x", 0, 0, tiled=True)
    pieces = (piece, passed_along(piece, "core", 1))

    g0 = gradient.astype(bf16)
    gm1 = passed_along(g0, "row", 1)
    gm4 = passed_along(g0, "row", 4)
    g4 = passed_along(g0, "row", -4)
    g6 = passed_along(gm1, "row", -7)

    g0 = gradient.astype(bf16)
    gm1 = passed_along(g0, "row", 1)
    gm4 = passed_along(g0, "row", 4)
    g4 = passed_along(g0, "row", -4)
    g6 = passed_along(gm1, "row", -7)
    g0, gm1, gm4, g4, g6 = blocks = lax.optimization_barrier((g0, gm1, gm4, g4, g6))
    chunks = (nx * nzh, full, lanes)
    (early,) = call(early_gram, [((len(EARLY), rows, rows), bf16)], (g0,), flops=HIDES)
    keep, give = call(
        late_gram,
        [(chunks, bf16)] * 2,
        (*blocks, early),
        [pltpu.VMEM((len(TILES) * rows + 8, lanes), f32)],
        flops=HIDES,
    )
    came = passed_along(give, "core", 1)

    shape = g0.shape
    tiles, out6 = call(
        assemble,
        [((len(TILES), rows, rows), bf16), (shape, bf16)],
        (*pieces, g0, gm1, g4),
        [pltpu.VMEM((len(TILES) * rows, rows), f32)],
        flops=3 * product,
    )
    came, tiles, out6 = lax.optimization_barrier((came, tiles, out6))
    out4, outm4, outm1 = call(
        functools.partial(products, (4, -4, -1)),
        [(shape, bf16), (shape, bf16), (shape, f32)],
        (tiles, *blocks),
        flops=9 * product,
    )
    came4, camem4 = passed_along(out4, "row", 4), passed_along(outm4, "row", -4)
    chained = (outm1 + passed_along(out6, "row", 7).astype(f32)).astype(bf16)
    camem1 = passed_along(chained, "row", -1)
    sent = (keep.astype(f32) + came.astype(f32)).astype(bf16).reshape(nx, nzh, full, lanes)
    got = lax.all_to_all(sent, "x", 0, 0, tiled=True)
    mine, sent = call(x_sum, [((2, full, lanes), bf16)] * 2, (got,))
    mine = (mine.astype(f32) + traded(sent, 0).astype(f32)).astype(bf16)
    total = (mine[0].astype(f32) + traded(mine[1], 1).astype(f32)).astype(bf16)
    total, camem1, came4, camem4 = lax.optimization_barrier((total, camem1, came4, camem4))
    one, two = (lax.ppermute(total, ALL, [(b, a) for a, b in pairs(pick, 0)]) for pick in (2, 3))
    one, two = one[:shard, :rows], two[:shard, :rows]
    share = jnp.where(place_in_shard < cut, one, two).astype(f32).T
    statistic = 0.9 * previous + 0.1 / INTER * share
    (out0,) = call(functools.partial(products, (0,)), [(shape, f32)], (tiles, *blocks), flops=4 * product)
    applied = out0 + came4.astype(f32) + camem4.astype(f32) + camem1.astype(f32)
    return (statistic, applied)


def solution(mesh):
    split = Mesh(mesh.devices.reshape(mesh.shape["row"], 4, 4, 2), ALL)
    spec = P("row", COL)
    return jax.shard_map(
        local, mesh=split, in_specs=(spec,) * 3, out_specs=(spec,) * 2, check_vma=False
    )
```

```python
import functools

import jax
import jax.numpy as jnp
from jax import lax
from jax.experimental import pallas as pl
from jax.experimental.pallas import tpu as pltpu
from jax.sharding import Mesh
from jax.sharding import PartitionSpec as P

INTER = 25600
COL = ("x", "zh", "core")
ALL = ("row",) + COL
TILES = ((0, 0), (0, -1), (6, 4), (-1, -4), (4, 0), (4, -1), (6, 0), (6, -1), (4, -4))
HIDES = 10**10


def passed_along(x, axis, by):
    count = lax.axis_size(axis)
    return lax.ppermute(x, axis, [(i, (i + by) % count) for i in range(count)])


def shard_routes(sizes, shard, tile):
    nx, nzh, ncore = sizes
    routes = []
    for c in range(nx * nzh * ncore):
        first, last = c * shard // tile, (c * shard + shard - 1) // tile
        core, rest = divmod(c, nx * nzh)
        x, zh = divmod(rest, nzh)
        place = (x * nzh + zh) * ncore + core
        one, two = TILES[first][0], TILES[last][0]
        routes.append((c, place, one, two, last * tile - c * shard if one != two else shard))
    return routes


def dot(left, right, dims):
    return lax.dot_general(left, right, (dims, ((), ())), preferred_element_type=jnp.float32)


def call(kernel, outs, args, scratch=(), flops=0):
    moved = sum(a.size * a.dtype.itemsize for a in args)
    return pl.pallas_call(
        kernel,
        out_shape=[jax.ShapeDtypeStruct(s, d) for s, d in outs],
        in_specs=[pl.BlockSpec(memory_space=pltpu.VMEM)] * len(args),
        out_specs=[pl.BlockSpec(memory_space=pltpu.VMEM)] * len(outs),
        scratch_shapes=list(scratch),
        cost_estimate=pl.CostEstimate(flops=flops, bytes_accessed=moved, transcendentals=0),
        compiler_params=pltpu.CompilerParams(vmem_limit_bytes=24 * 2**20),
    )(*args)


def gram(g0, gm1, gm4, g4, g6, keep, give, flat):
    held = {0: g0, -1: gm1, -4: gm4, 4: g4, 6: g6}
    core = lax.axis_index("core")
    rows = g0.shape[0]
    count, full, _ = keep.shape
    shard = len(TILES) * rows // (2 * count)
    for k, (a, b) in enumerate(TILES):
        flat[k * rows : (k + 1) * rows, :rows] = dot(held[b][...], held[a][...], ((1,), (1,)))

    def put(outs):
        for q in range(count):
            for b, out in enumerate(outs):
                start = (2 * q + b) * shard
                out[q] = flat[start : start + full].astype(out.dtype)

    @pl.when(core == 0)
    def _():
        put((keep, give))

    @pl.when(core == 1)
    def _():
        put((give, keep))


def core_sum(keep, came, out):
    for q in range(out.shape[0]):
        out[q] = (keep[q].astype(jnp.float32) + came[q].astype(jnp.float32)).astype(out.dtype)


def partner(zh, core, turn):
    first = (core + turn) % 2 == 0
    near, far = zh + 1 - 2 * (zh % 2), 3 - zh
    if isinstance(core, int):
        return near if first else far
    return jnp.where(first, near, far)


def x_sum(came, keep, send):
    zh, core = lax.axis_index("zh"), lax.axis_index("core")
    for out, who in ((keep, zh), (send, partner(zh, core, 0))):
        for n, q in enumerate((who, partner(who, core, 1))):
            total = sum(came[p, q].astype(jnp.float32) for p in range(came.shape[0]))
            out[n] = total.astype(out.dtype)


def assemble(mine, other, g0, gm1, g4, tiles, out6, flat):
    nx, nzh = mine.shape[:2]
    rows = tiles.shape[1]
    shard = flat.shape[0] // (2 * nx * nzh)
    core = lax.axis_index("core")

    def put(parts):
        for x in range(nx):
            for zh in range(nzh):
                for b, part in enumerate(parts):
                    start = ((x * nzh + zh) * 2 + b) * shard
                    flat[start : start + shard] = part[x, zh].astype(jnp.float32)[:shard, :rows]

    @pl.when(core == 0)
    def _():
        put((mine, other))

    @pl.when(core == 1)
    def _():
        put((other, mine))

    for k in range(len(TILES)):
        tiles[k] = flat[k * rows : (k + 1) * rows].astype(tiles.dtype)
    out6[...] = summed_terms(tiles, {0: g0, -1: gm1, 4: g4}, 6).astype(out6.dtype)


def summed_terms(tiles, held, o):
    total = None
    for k, (a, b) in enumerate(TILES):
        if a == o:
            term = dot(tiles[k], held[b][...], ((0,), (0,)))
            total = term if total is None else total + term
        if b == o and 0 < k < len(TILES) - 1:
            term = dot(tiles[k], held[a][...], ((1,), (0,)))
            total = term if total is None else total + term
    return total


def products(which, tiles, g0, gm1, gm4, g4, g6, *outs):
    held = {0: g0, -1: gm1, -4: gm4, 4: g4, 6: g6}
    for o, out in zip(which, outs):
        out[...] = summed_terms(tiles, held, o).astype(out.dtype)


def local(gradient, previous, root):
    rows, shard = previous.shape
    n_row = lax.axis_size("row")
    nx, nzh, ncore = (lax.axis_size(a) for a in COL)
    n_col = nx * nzh * ncore
    routes = shard_routes((nx, nzh, ncore), shard, rows)
    cuts = jnp.asarray([r[4] for r in routes], jnp.int32)
    cut = cuts[lax.axis_index(COL)]
    place_in_shard = lax.broadcasted_iota(jnp.int32, (shard, rows), 0)
    bf16, f32 = jnp.bfloat16, jnp.float32
    product = 2 * rows * rows * gradient.shape[1]

    def pairs(pick, place):
        return [
            ((i + r[pick]) % n_row * n_col + r[0], i * n_col + r[place])
            for i in range(n_row)
            for r in routes
            if pick == 2 or r[2] != r[3]
        ]

    mine = root.T
    one = lax.ppermute(mine, ALL, pairs(2, 0))
    two = lax.ppermute(mine, ALL, pairs(3, 0))
    one, two, gradient = lax.optimization_barrier((one, two, gradient))
    piece = jnp.where(place_in_shard < cut, one, two)
    full, lanes = -(-shard // 16) * 16, -(-rows // 128) * 128
    piece = jnp.pad(piece, ((0, full - shard), (0, lanes - rows)))
    turns = [
        [(zh * ncore + c, partner(zh, c, turn) * ncore + c) for zh in range(nzh) for c in range(ncore)]
        for turn in (0, 1)
    ]

    def traded(x, turn):
        return lax.ppermute(x, ("zh", "core"), turns[turn])

    piece = lax.all_to_all(jnp.broadcast_to(piece[None], (nzh,) + piece.shape), "zh", 0, 0, tiled=True)
    piece = lax.all_to_all(jnp.broadcast_to(piece[None], (nx,) + piece.shape), "x", 0, 0, tiled=True)

    g0 = gradient.astype(bf16)
    gm1 = passed_along(g0, "row", 1)
    gm4 = passed_along(g0, "row", 4)
    g4 = passed_along(g0, "row", -4)
    g6 = passed_along(gm1, "row", -7)

    g0 = gradient.astype(bf16)
    gm1 = passed_along(g0, "row", 1)
    gm4 = passed_along(g0, "row", 4)
    g4 = passed_along(g0, "row", -4)
    g6 = passed_along(gm1, "row", -7)
    g0, gm1, gm4, g4, g6 = blocks = lax.optimization_barrier((g0, gm1, gm4, g4, g6))
    chunks = (nx * nzh, full, lanes)
    keep, give = call(
        gram,
        [(chunks, bf16)] * 2,
        blocks,
        [pltpu.VMEM((len(TILES) * rows + 8, lanes), f32)],
        flops=HIDES,
    )
    give, piece = lax.optimization_barrier((give, piece))
    came = passed_along(give, "core", 1)
    pieces = (piece, passed_along(piece, "core", 1))

    shape = g0.shape
    tiles, out6 = call(
        assemble,
        [((len(TILES), rows, rows), bf16), (shape, bf16)],
        (*pieces, g0, gm1, g4),
        [pltpu.VMEM((len(TILES) * rows, rows), f32)],
        flops=3 * product,
    )
    out4, outm4, outm1 = call(
        functools.partial(products, (4, -4, -1)),
        [(shape, bf16), (shape, bf16), (shape, f32)],
        (tiles, *blocks),
        flops=9 * product,
    )
    came4, camem4 = passed_along(out4, "row", 4), passed_along(outm4, "row", -4)
    chained = (outm1 + passed_along(out6, "row", 7).astype(f32)).astype(bf16)
    camem1 = passed_along(chained, "row", -1)
    (sent,) = call(core_sum, [(chunks, bf16)], (keep, came), flops=HIDES)
    sent = sent.reshape(nx, nzh, full, lanes)
    got = lax.all_to_all(sent, "x", 0, 0, tiled=True)
    mine, sent = call(x_sum, [((2, full, lanes), bf16)] * 2, (got,))
    mine = (mine.astype(f32) + traded(sent, 0).astype(f32)).astype(bf16)
    mine, came4, camem4 = lax.optimization_barrier((mine, came4, camem4))
    halves = []
    for pick in (2, 3):
        parts = []
        for n in (0, 1):
            route = []
            for i in range(n_row):
                for r in routes:
                    x_zh, c = divmod(r[0], ncore)
                    x, zh = divmod(x_zh, nzh)
                    source = (x * nzh + (partner(zh, c, 1) if n else zh)) * ncore + c
                    if pick == 2 or r[2] != r[3]:
                        route.append((i * n_col + source, (i + r[pick]) % n_row * n_col + r[0]))
            parts.append(lax.ppermute(mine[n], ALL, route)[:shard, :rows].astype(f32))
        halves.append(parts[0] + parts[1])
    one, two = halves
    share = jnp.where(place_in_shard < cut, one, two).T
    statistic = 0.9 * previous + 0.1 / INTER * share
    (out0,) = call(functools.partial(products, (0,)), [(shape, f32)], (tiles, *blocks), flops=4 * product)
    applied = out0 + came4.astype(f32) + camem4.astype(f32) + camem1.astype(f32)
    return (statistic, applied)


def solution(mesh):
    split = Mesh(mesh.devices.reshape(mesh.shape["row"], 4, 4, 2), ALL)
    spec = P("row", COL)
    return jax.shard_map(
        local, mesh=split, in_specs=(spec,) * 3, out_specs=(spec,) * 2, check_vma=False
    )
```
